256 devices in a mesh: section: 4 (over y_lo, core), dp: 8 (over z), expert: 8 (over x, y_hi).
Axes of the slice: x: 4, y: 4 (y_hi: 2, y_lo: 2; y = y_hi * 2 + y_lo), z: 8, core: 2. Of those that a mesh axis runs over, the one named last changes fastest.
Arguments:
- grad_out: bfloat16 [4, 8192, 3072], P('section', ('dp', 'expert')), may hold values from -6 to 6
- expert_ids: int32 [4, 8192, 2], P('section', ('dp', 'expert')), may hold values from 0 to 7, as said below
- slot_ids: int32 [4, 8192, 2], P('section', ('dp', 'expert')), may hold values from 0 to 35, as said below
- gates: float32 [4, 8192, 2], P('section', ('dp', 'expert')), may hold values from 0.1 to 1
- hidden: bfloat16 [4, 2304, 32768], P('section', None, ('dp', 'expert')), may hold values from -0.3984375 to 0.3984375
- w_down: bfloat16 [4, 32768, 3072], P('section', ('dp', 'expert')), may hold values from -0.0625 to 0.0625
Outputs:
- hidden_grad: bfloat16 [4, 2304, 32768], P('section', None, ('dp', 'expert'))
- weight_grad: bfloat16 [4, 32768, 3072], P('section', ('dp', 'expert'))
The draws below stay inside these ranges and needn't reach their ends.
Inputs may be any that keep to these rules, and one draw needn't show every extreme that they name: `expert_ids`: each token names 2 different experts. Within one block of 128 rows at most 36 routes go to one expert, and in every section one expert below 4 receives exactly 36 routes from each of its 64 blocks. `slot_ids`: the routes of one block to one expert take the slots 0 to their count minus one, each once.
All inputs are finite; a program needn't handle non-finite values.
Results may differ from the reference program's by a relative error of at most 0.0049.
Values may be sent and summed in bfloat16 or wider, within the bound.
A program may use at most 128 MiB of HBM per device.

```python
import jax
import jax.numpy as jnp
from jax import lax

D = 3072
FF = 8192
TOP = 2
EXPERTS = 8
FLIGHT = 4
TOK_DEV = 128
SECTIONS = 4
SOURCES = 64
TOKENS = 8192
CAP = 36
SLOTS = 2304


def route_tables(key):
    block_count = SECTIONS * SOURCES
    key_full, key_move, key_order = jax.random.split(key, 3)
    fullest = jax.random.randint(key_full, (SECTIONS,), 0, FLIGHT)
    fullest = jnp.repeat(fullest, SOURCES)
    others = EXPERTS - 1
    remaining = TOK_DEV * TOP - CAP
    base_count = remaining // others
    overflow_excess = remaining - base_count * others
    spread = max(0, min(base_count, CAP - base_count - 1) // 2)
    pair_count = others // 2
    rest_counts = base_count + (jnp.arange(others) < overflow_excess).astype(jnp.int32)
    rest_counts = jnp.tile(rest_counts[None, :], (block_count, 1))
    if pair_count > 0:
        moves = jax.random.randint(key_move, (block_count, pair_count), -spread, spread + 1)
        rest_counts = rest_counts.at[:, 0:2 * pair_count:2].add(moves)
        rest_counts = rest_counts.at[:, 1:2 * pair_count:2].add(-moves)
    labels = jnp.arange(EXPERTS, dtype=jnp.int32)
    expert_tallies = CAP * (labels[None, :] == fullest[:, None]).astype(jnp.int32)
    for other in range(others):
        target = (fullest + 1 + other) % EXPERTS
        expert_tallies = expert_tallies + rest_counts[:, other:other + 1] * (labels[None, :] == target[:, None]).astype(jnp.int32)
    ends = jnp.cumsum(expert_tallies, axis=1)
    starts = ends - expert_tallies
    route_position = jnp.arange(TOK_DEV * TOP, dtype=jnp.int32)
    chosen = jnp.sum((route_position[None, :, None] >= ends[:, None, :]).astype(jnp.int32), axis=2)
    ranks = route_position[None, :] - jnp.take_along_axis(starts, chosen, axis=1)
    chosen = chosen.reshape(block_count, TOP, TOK_DEV)
    ranks = ranks.reshape(block_count, TOP, TOK_DEV)
    order_keys = jax.random.split(key_order, block_count)
    orders = jax.vmap(lambda single: jax.random.permutation(single, TOK_DEV))(order_keys)
    orders = jnp.broadcast_to(orders[:, None, :], (block_count, TOP, TOK_DEV))
    chosen = jnp.take_along_axis(chosen, orders, axis=2).transpose(0, 2, 1)
    ranks = jnp.take_along_axis(ranks, orders, axis=2).transpose(0, 2, 1)
    return (chosen.reshape(SECTIONS, TOKENS, TOP), ranks.reshape(SECTIONS, TOKENS, TOP))


def draw_expert_ids(key, part):
    return route_tables(key)[0].astype(jnp.int32)


def draw_slot_ids(key, part):
    return route_tables(key)[1].astype(jnp.int32)


def block_levels(own_key, dims, pieces, smallest, high):
    def one(axis_at, parts):
        heights = jax.random.uniform(jax.random.fold_in(jax.random.fold_in(own_key, 6), axis_at), (parts,), jnp.float32, smallest / len(pieces), high / len(pieces))
        return jnp.repeat(jnp.exp(heights), dims[axis_at] // parts).reshape((-1,) + (1,) * (len(dims) - axis_at - 1))

    factor_of = one(*pieces[0])
    for cut in pieces[1:]:
        factor_of = factor_of * one(*cut)
    return factor_of


def normal_values(rng, extent, width, most, pieces=(), kind=jnp.bfloat16):
    level = block_levels(rng, extent, pieces, -0.22, 0.18) if pieces else 1.0
    values = jax.random.normal(rng, extent, jnp.float32) * width * level
    return jnp.minimum(jnp.maximum(values, -most), most).astype(kind)


def setup_inputs(seed: int = 0) -> dict:
    key_list = jax.random.split(jax.random.key(seed), 7)
    return {
        "grad_out": normal_values(key_list[0], (SECTIONS, TOKENS, D), 1.0, 6.0, ((0, 4), (1, 64))),
        "expert_ids": draw_expert_ids(jax.random.fold_in(key_list[6], 71), 0),
        "slot_ids": draw_slot_ids(jax.random.fold_in(key_list[6], 71), 0),
        "gates": jnp.clip(0.1 + 0.9 * jax.random.uniform(key_list[3], (SECTIONS, TOKENS, TOP), jnp.float32) ** block_levels(key_list[3], (SECTIONS, TOKENS, TOP), ((0, 4), (1, 64)), -0.2, 0.2), 0.1, 1.0),
        "hidden": normal_values(key_list[4], (SECTIONS, SLOTS, FLIGHT * FF), 0.05, 0.3984375, ((0, 4), (2, 64))),
        "w_down": normal_values(key_list[5], (SECTIONS, FLIGHT * FF, D), FF ** -0.5, 0.0625, ((0, 4), (1, 64))),
    }


def reference(grad_out, expert_ids, slot_ids, gates, hidden, w_down):
    scaled = (gates[..., None] * grad_out[:, :, None, :].astype(jnp.float32)).astype(jnp.bfloat16)
    routes = scaled.reshape(SECTIONS, SOURCES, TOK_DEV * TOP, D)
    slot_index = (expert_ids * CAP + slot_ids).astype(jnp.int32).reshape(SECTIONS, SOURCES, TOK_DEV * TOP)
    labels = jnp.arange(FLIGHT * CAP, dtype=jnp.int32)

    def place(operands):
        routes_per_section, section_index = operands
        indicator_matrix = (section_index[..., None] == labels).astype(jnp.float32)
        return jnp.einsum("vze,vzj->vej", indicator_matrix, routes_per_section.astype(jnp.float32)).astype(jnp.bfloat16)

    placed = lax.map(place, (routes, slot_index))
    placed = placed.reshape(SECTIONS, SOURCES, FLIGHT, CAP, D).transpose(0, 2, 1, 3, 4)
    dispatched = placed.reshape(SECTIONS * FLIGHT, SLOTS, D)
    saved_all = hidden.reshape(SECTIONS, SLOTS, FLIGHT, FF).transpose(0, 2, 1, 3).reshape(SECTIONS * FLIGHT, SLOTS, FF)
    weights_all = w_down.reshape(SECTIONS * FLIGHT, FF, D)

    def one_expert(operands):
        slot_grad, saved, projection = operands
        section_part = jnp.dot(slot_grad, projection.T, preferred_element_type=jnp.float32).astype(jnp.bfloat16)
        weight_part = jnp.dot(saved.T, slot_grad, preferred_element_type=jnp.float32).astype(jnp.bfloat16)
        return section_part, weight_part

    section_grad, weight_grad = lax.map(one_expert, (dispatched, saved_all, weights_all))
    section_grad = section_grad.reshape(SECTIONS, FLIGHT, SLOTS, FF).transpose(0, 2, 1, 3).reshape(SECTIONS, SLOTS, FLIGHT * FF)
    weight_grad = weight_grad.reshape(SECTIONS, FLIGHT * FF, D)
    hidden_grad = jnp.concatenate([section_grad[1:], jnp.zeros_like(section_grad[:1])], axis=0)
    return hidden_grad, weight_grad
```

```python
import functools

import jax
import jax.numpy as jnp
from jax import lax
from jax.experimental import pallas as pl
from jax.experimental.pallas import tpu as pltpu
from jax.sharding import PartitionSpec as P

MESH = pl.DeviceIdType.MESH
FLIGHT = 4
BF16, F32, I32 = jnp.bfloat16, jnp.float32, jnp.int32

D = 3072
CAP = 36
BAND = 16
TAIL = CAP - 2 * BAND
QUARTER = D // 4
WIDTH = 2 * D + QUARTER
UNITS = 512
BLOCKS = 8
PLANE = 8
ROWS = PLANE * CAP
SLOTS = BLOCKS * ROWS
MAIN = PLANE * 2 * BAND
TAILS = PLANE * TAIL
HALF_A = 17 * 128
HALF_B = (WIDTH - 2 * HALF_A) // 2
A_ALL = (0, 2 * HALF_A)
A_0 = (0, HALF_A)
A_1 = (HALF_A, HALF_A)
B_ALL = (2 * HALF_A, 2 * HALF_B)
B_0 = (2 * HALF_A, HALF_B)
B_1 = (2 * HALF_A + HALF_B, HALF_B)
SEM_OF = {A_ALL: 0, A_0: 0, A_1: 1, B_ALL: 2, B_0: 2, B_1: 3}


def iota(shape, dim):
    return lax.broadcasted_iota(I32, shape, dim)


def onehot(cond):
    return cond.astype(F32).astype(BF16)


def dot(a, b, dims=((1,), (0,))):
    return lax.dot_general(a, b, (dims, ((), ())), preferred_element_type=F32)


def kernel(ids_ref, slots_ref, gates_ref, grad_hbm, hid_hbm, w_hbm, hout, wout,
           arr, outg, grad, hid, w, hmain, htail, utail, acc, sec, wbuf,
           in_sem, loc_sem, out_sem, send_sem, recv_sem, hsend_sem, hrecv_sem):
    section = lax.axis_index("section")
    z = lax.axis_index("dp")
    xy = lax.axis_index("expert")
    x, yh = lax.div(xy, 2), lax.rem(xy, 2)
    zb = lax.rem(z, 2)
    e = lax.div(z, 2)
    sg = 2 * zb - 1

    grad_in = pltpu.make_async_copy(grad_hbm, grad, in_sem.at[0])
    grad_in.start()
    hid_in = pltpu.make_async_copy(hid_hbm, hid, in_sem.at[1])
    hid_in.start()
    w_in = pltpu.make_async_copy(w_hbm, w, in_sem.at[2])
    w_in.start()

    def device(dz, dx, flip, ds=0):
        to_y = 1 - yh if flip else yh
        return (section + ds, lax.rem(z + dz + 8, 8), lax.rem(x + dx + 4, 4) * 2 + to_y)

    zflip = 1 - 2 * zb
    to_z = device(zflip, 0, False)
    to_y = device(0, 0, True)
    to_right = device(0, 1, False)
    to_left = device(0, -1, False)
    transit = {1: device(sg, 0, False), 2: device(-2 * sg, 0, False), 3: device(3 * sg, 0, False)}
    transit_from = {1: transit[1], 2: device(2 * sg, 0, False), 3: transit[3]}

    barrier = pltpu.get_barrier_semaphore()
    after = (lax.rem(section + 1, 4), z, xy)
    for other in (to_z, to_y, to_right, to_left, transit_from[1], transit_from[2], transit_from[3], after):
        pl.semaphore_signal(barrier, inc=1, device_id=other, device_id_type=MESH)

    def chunk_expert(j):
        return lax.rem(e + {0: 0, 1: sg, 2: -sg, 3: 2}[j] + 4, 4)

    experts = [chunk_expert(j) for j in range(4)]

    def expert_rows(j):
        base = jnp.full(j.shape, experts[3] * CAP, I32)
        for k in (2, 1, 0):
            base = jnp.where(j == k, experts[k] * CAP, base)
        return base

    place = ids_ref[...] * CAP + slots_ref[...]
    place0, place1 = place[0:1, :], place[1:2, :]
    gate0, gate1 = gates_ref[0:1, :], gates_ref[1:2, :]
    m = iota((128, 1), 0)
    want = expert_rows((m >> 4) & 3) + 16 * (m >> 6) + (m & 15)
    hit0, hit1 = place0 == want, place1 == want
    pick_main = onehot(hit0 | hit1)
    gate_main = jnp.sum(jnp.where(hit0, gate0, 0.0) + jnp.where(hit1, gate1, 0.0), axis=1, keepdims=True)
    m = iota((64, 1), 0)
    quarter = (m >> 2) & 3
    want = expert_rows(m >> 4) + 2 * BAND + (m & 3)
    hit0, hit1 = place0 == want, place1 == want
    tail_hit = hit0 | hit1
    gate_tail = jnp.sum(jnp.where(hit0, gate0, 0.0) + jnp.where(hit1, gate1, 0.0), axis=1, keepdims=True)

    def slot_of(j, dx=0, fy=False, fz=False):
        tz = z + zflip if fz else z
        tsg = -sg if fz else sg
        ty = 1 - yh if fy else yh
        return lax.rem(tz + tsg * j + 8, 8) * PLANE + lax.rem(x + dx + 4, 4) * 2 + ty

    mine = slot_of(0)
    grad_in.wait()
    for h in range(2):
        for c in range(0, D, 512):
            part = dot(pick_main[64 * h:64 * h + 64, :], grad[:, c:c + 512])
            part = (part * gate_main[64 * h:64 * h + 64, :]).astype(BF16)
            arr[mine, :, h * D + c:h * D + c + 512] = part[0:16]
            for j in (1, 2, 3):
                outg[j - 1, :, h * D + c:h * D + c + 512] = part[16 * j:16 * j + 16]
    part = jnp.zeros((64, QUARTER), F32)
    for q in range(4):
        part += dot(onehot(tail_hit & (quarter == q)), grad[:, q * QUARTER:(q + 1) * QUARTER])
    part = (part * gate_tail).astype(BF16)
    arr[mine, :, 2 * D:WIDTH] = part[0:16]
    for j in (1, 2, 3):
        outg[j - 1, :, 2 * D:WIDTH] = part[16 * j:16 * j + 16]

    pl.semaphore_wait(barrier, 8)

    sends = []

    def copy_of(slot, cols, to, n):
        piece = arr.at[slot, :, pl.ds(cols[0], cols[1])]
        return pltpu.make_async_remote_copy(
            src_ref=piece, dst_ref=piece, send_sem=send_sem.at[n],
            recv_sem=recv_sem.at[slot, SEM_OF[cols]], device_id=to, device_id_type=MESH)

    def send(slot, cols, to):
        copy = copy_of(slot, cols, to, len(sends))
        copy.start()
        sends.append(copy)

    def landed(slot, cols):
        copy_of(slot, cols, to_z, 0).wait_recv()

    def send_transit(j):
        copy = pltpu.make_async_remote_copy(
            src_ref=outg.at[j - 1], dst_ref=arr.at[mine], send_sem=send_sem.at[len(sends)],
            recv_sem=recv_sem.at[mine, 0], device_id=transit[j], device_id_type=MESH)
        copy.start()
        sends.append(copy)

    def wait_transit(j):
        slot = slot_of(j)
        pltpu.make_async_remote_copy(
            src_ref=outg.at[0], dst_ref=arr.at[slot], send_sem=send_sem.at[0],
            recv_sem=recv_sem.at[slot, 0], device_id=to_z, device_id_type=MESH).wait_recv()

    def stage0(j):
        if j:
            wait_transit(j)
        send(slot_of(j), A_ALL, to_z)
        send(slot_of(j), B_ALL, to_right)
        send(slot_of(j), B_ALL, to_left)

    def stage1(j):
        landed(slot_of(j, fz=True), A_ALL)
        send(slot_of(j), A_ALL, to_y)
        send(slot_of(j, fz=True), A_ALL, to_y)
        landed(slot_of(j, dx=-1), B_ALL)
        send(slot_of(j, dx=-1), B_0, to_right)
        landed(slot_of(j, dx=1), B_ALL)
        send(slot_of(j, dx=1), B_1, to_left)

    def stage2(j):
        for fy in (False, True):
            for fz in (False, True):
                if fy:
                    landed(slot_of(j, fy=True, fz=fz), A_ALL)
                send(slot_of(j, fy=fy, fz=fz), A_ALL, to_right)
                send(slot_of(j, fy=fy, fz=fz), A_ALL, to_left)
        for dx in (0, -1, 1):
            send(slot_of(j, dx=dx), B_ALL, to_y)
        landed(slot_of(j, dx=2), B_0)
        landed(slot_of(j, dx=2), B_1)
        send(slot_of(j, dx=2), B_ALL, to_y)

    def stage3(j):
        for fy in (False, True):
            for fz in (False, True):
                landed(slot_of(j, dx=-1, fy=fy, fz=fz), A_ALL)
                send(slot_of(j, dx=-1, fy=fy, fz=fz), A_0, to_right)
                landed(slot_of(j, dx=1, fy=fy, fz=fz), A_ALL)
                send(slot_of(j, dx=1, fy=fy, fz=fz), A_1, to_left)
        for dx in (0, -1, 1, 2):
            send(slot_of(j, dx=dx), B_ALL, to_z)
        for dx in (0, -1, 1, 2):
            landed(slot_of(j, dx=dx, fy=True), B_ALL)
            send(slot_of(j, dx=dx, fy=True), B_ALL, to_z)

    def stage4(j):
        for fy in (False, True):
            for fz in (False, True):
                landed(slot_of(j, dx=2, fy=fy, fz=fz), A_0)
                landed(slot_of(j, dx=2, fy=fy, fz=fz), A_1)
            for dx in (0, -1, 1, 2):
                landed(slot_of(j, dx=dx, fy=fy, fz=True), B_ALL)

    v = iota((1, MAIN), 1)
    main_at = CAP * ((v >> 4) & 7) + BAND * (v >> 7) + (v & 15)
    perm_main = onehot(iota((ROWS, 1), 0) == main_at)
    u = iota((1, 128), 1)
    tail_at = CAP * ((u & 31) >> 2) + 2 * BAND + (u & 3)
    tail_match = iota((ROWS, 1), 0) == tail_at
    perm_tail = onehot(iota((ROWS, 1), 0) == tail_at)[:, 0:TAILS]

    def turn_hidden(b):
        rows = hid[ROWS * b:ROWS * b + ROWS, :]
        hmain[b] = dot(rows, perm_main, ((0,), (0,))).astype(BF16)
        spread = onehot(tail_match & ((u >> 5) == b % 4))
        part = dot(rows, spread, ((0,), (0,))).astype(BF16)
        cols = slice(128 * (b // 4), 128 * (b // 4) + 128)
        if b % 4 == 0:
            htail[:, cols] = part
        else:
            htail[:, cols] += part

    def plane_of(j, k):
        return lax.rem(2 * e + (8 - j if k == 0 else 1 + j), 8)

    t = iota((TAILS, 1), 0)
    vt = iota((1, 128), 1)
    pick_tail = [onehot(vt == 16 * (t >> 2) + 4 * q + (t & 3)) for q in range(4)]

    def unpack_tails(b):
        packed = arr[pl.ds(PLANE * b, PLANE), :, 2 * D:WIDTH].reshape(PLANE * BAND, QUARTER)
        at = pl.multiple_of(b * TAILS, TAILS)
        for q in range(4):
            utail[pl.ds(at, TAILS), q * QUARTER:(q + 1) * QUARTER] = dot(pick_tail[q], packed).astype(BF16)

    def band(b, h, c, n):
        return arr[pl.ds(PLANE * b, PLANE), :, h * D + c:h * D + c + n].reshape(PLANE * BAND, n)

    def hidden_copy(b):
        rows = pl.ds(pl.multiple_of(b * ROWS, ROWS), ROWS)
        return pltpu.make_async_remote_copy(
            src_ref=sec.at[rows], dst_ref=hout.at[rows], send_sem=hsend_sem.at[b],
            recv_sem=hrecv_sem.at[b], device_id=device(0, 0, False, -1), device_id_type=MESH)

    def section_part(b):
        at = pl.multiple_of(b * TAILS, TAILS)
        weight = w[...]
        dims = ((1,), (1,))
        low = dot(band(b, 0, 0, D), weight, dims).astype(BF16)
        high = dot(band(b, 1, 0, D), weight, dims).astype(BF16)
        tail = dot(utail[pl.ds(at, TAILS), :], weight, dims).astype(BF16)
        out = dot(perm_main[:, 0:128], low) + dot(perm_main[:, 128:256], high) + dot(perm_tail, tail)
        sec[pl.ds(pl.multiple_of(b * ROWS, ROWS), ROWS), :] = out.astype(BF16)
        hidden_copy(b).start()

    def weight_term(b, c, n):
        return (dot(hmain[b, :, 0:128], band(b, 0, c, n))
                + dot(hmain[b, :, 128:256], band(b, 1, c, n)))

    def compute(j, first, last):
        planes = [plane_of(j, k) for k in (0, 1)]
        for b in planes:
            unpack_tails(b)

        @pl.when(section > 0)
        def _():
            for b in planes:
                section_part(b)

        for c in range(0, D, 512):
            part = weight_term(planes[0], c, 512) + weight_term(planes[1], c, 512)
            if not first:
                part += acc[:, c:c + 512]
            if not last:
                acc[:, c:c + 512] = part
            else:
                part += dot(htail[...], utail[:, c:c + 512])
                wbuf[:, c:c + 512] = part.astype(BF16)
                pltpu.make_async_copy(wbuf.at[:, c:c + 512], wout.at[:, c:c + 512], out_sem.at[c // 512]).start()

    stage0(0)
    for j in (1, 2, 3):
        send_transit(j)
    hid_in.wait()
    for b in range(4):
        turn_hidden(b)
    stage1(0)
    stage0(1)
    for b in range(4, 8):
        turn_hidden(b)
    w_in.wait()
    stage2(0)
    stage1(1)
    stage0(2)
    stage2(1)
    stage3(0)
    stage1(2)
    stage0(3)
    stage2(2)
    stage3(1)
    stage1(3)
    stage2(3)
    stage4(0)
    compute(0, True, False)
    stage3(2)
    stage4(1)
    compute(1, False, False)
    stage3(3)
    stage4(2)
    compute(2, False, False)
    stage4(3)
    compute(3, False, True)

    @pl.when(section == 3)
    def _():
        hid[...] = jnp.zeros((SLOTS, UNITS), BF16)
        zero = pltpu.make_async_copy(hid, hout, loc_sem)
        zero.start()
        zero.wait()

    for c in range(0, D, 512):
        pltpu.make_async_copy(wbuf.at[:, c:c + 512], wout.at[:, c:c + 512], out_sem.at[c // 512]).wait()
    for copy in sends:
        copy.wait_send()

    @pl.when(section > 0)
    def _():
        for b in range(BLOCKS):
            hidden_copy(b).wait_send()

    @pl.when(section < 3)
    def _():
        for b in range(BLOCKS):
            hidden_copy(b).wait_recv()


def body(grad_out, expert_ids, slot_ids, gates, hidden, w_down):
    anywhere = pl.BlockSpec(memory_space=pl.ANY)
    vmem = pl.BlockSpec(memory_space=pltpu.VMEM)
    dma = pltpu.SemaphoreType.DMA
    hout, wout = pl.pallas_call(
        kernel,
        out_shape=(jax.ShapeDtypeStruct((SLOTS, UNITS), BF16), jax.ShapeDtypeStruct((UNITS, D), BF16)),
        in_specs=[vmem] * 3 + [anywhere] * 3,
        out_specs=(anywhere, anywhere),
        scratch_shapes=[
            pltpu.VMEM((BLOCKS * PLANE, BAND, WIDTH), BF16),
            pltpu.VMEM((3, BAND, WIDTH), BF16),
            pltpu.VMEM((128, D), BF16),
            pltpu.VMEM((SLOTS, UNITS), BF16),
            pltpu.VMEM((UNITS, D), BF16),
            pltpu.VMEM((BLOCKS, UNITS, MAIN), BF16),
            pltpu.VMEM((UNITS, BLOCKS * TAILS), BF16),
            pltpu.VMEM((BLOCKS * TAILS, D), BF16),
            pltpu.VMEM((UNITS, D), F32),
            pltpu.VMEM((SLOTS, UNITS), BF16),
            pltpu.VMEM((UNITS, D), BF16),
            dma((3,)), dma, dma((6,)), dma((160,)), dma((64, 4)), dma((8,)), dma((8,)),
        ],
        compiler_params=pltpu.CompilerParams(
            collective_id=0, has_side_effects=True, vmem_limit_bytes=56 * 2**20),
        cost_estimate=pl.CostEstimate(flops=15 * 10**9, bytes_accessed=12 * 10**6, transcendentals=0),
        name="dispatch_and_products",
    )(expert_ids[0].T, slot_ids[0].T, gates[0].T, grad_out[0], hidden[0], w_down[0])
    return (hout[None], wout[None])


def solution(mesh):
    in_specs = (
        P("section", ("dp", "expert"), None),
        P("section", ("dp", "expert"), None),
        P("section", ("dp", "expert"), None),
        P("section", ("dp", "expert"), None),
        P("section", None, ("dp", "expert")),
        P("section", ("dp", "expert"), None),
    )
    out_specs = (P("section", None, ("dp", "expert")), P("section", ("dp", "expert"), None))
    return jax.shard_map(body, mesh=mesh, in_specs=in_specs, out_specs=out_specs, check_vma=False)
```

```python
import functools

import jax
import jax.numpy as jnp
from jax import lax
from jax.experimental import pallas as pl
from jax.experimental.pallas import tpu as pltpu
from jax.sharding import PartitionSpec as P

MESH = pl.DeviceIdType.MESH
FLIGHT = 4
BF16, F32, I32 = jnp.bfloat16, jnp.float32, jnp.int32

D = 3072
CAP = 36
BAND = 16
TAIL = CAP - 2 * BAND
QUARTER = D // 4
WIDTH = 2 * D + QUARTER
UNITS = 512
BLOCKS = 8
PLANE = 8
ROWS = PLANE * CAP
SLOTS = BLOCKS * ROWS
MAIN = PLANE * 2 * BAND
TAILS = PLANE * TAIL
SECTION_STEP = 768
HALF_A = 16 * 128
HALF_B = (WIDTH - 2 * HALF_A) // 2
A_ALL = (0, 2 * HALF_A)
A_0 = (0, HALF_A)
A_1 = (HALF_A, HALF_A)
B_ALL = (2 * HALF_A, 2 * HALF_B)
B_0 = (2 * HALF_A, HALF_B)
B_1 = (2 * HALF_A + HALF_B, HALF_B)
ORDER = (
    ("A2", 0, 0), ("B3", 0, 0), ("A1", 0), ("T1",), ("T2",), ("B1R", 0), ("B1L", 0), ("A3R", 0, 0, 0),
    ("A3L", 0, 0, 0), ("B4", 0, 0, 0), ("H", 0), ("H", 1), ("H", 2), ("H", 3), ("H", 4), ("H", 5), ("H", 6),
    ("H", 7), ("B4", 0, 0, 1), ("B3", 0, -1), ("B3", 0, 1), ("B2R", 0), ("B2L", 0), ("A3R", 0, 1, 0),
    ("A3L", 0, 1, 0), ("A4R", 0, 0, 0), ("A4L", 0, 0, 0), ("B4", 0, -1, 0), ("B4", 0, 1, 0), ("B3", 0, 2), ("T3",),
    ("A2", 0, 1), ("A3R", 0, 0, 1), ("A3L", 0, 0, 1), ("A2", 1, 0), ("B1R", 1), ("B1L", 1), ("A3R", 1, 0, 0),
    ("A3L", 1, 0, 0), ("B3", 1, 0), ("B4", 0, -1, 1), ("B4", 0, 1, 1), ("A4R", 0, 1, 0), ("A4L", 0, 1, 0),
    ("B3", 1, -1), ("B2R", 1), ("B4", 0, 2, 0), ("B2L", 1), ("B3", 1, 1), ("A4R", 0, 0, 1), ("A4L", 0, 0, 1),
    ("A2", 2, 0), ("A3R", 0, 1, 1), ("A3L", 0, 1, 1), ("A3R", 1, 1, 0), ("A3L", 1, 1, 0), ("C", 0, 0, 0),
    ("B3", 1, 2), ("B4", 0, 2, 1), ("B3", 2, 0), ("C", 0, 0, 1), ("A1", 1), ("A4R", 1, 0, 0), ("A4L", 1, 0, 0),
    ("C", 0, 0, 2), ("C", 0, 0, 3), ("B4", 1, 0, 0), ("B1R", 2), ("B1L", 2), ("A3R", 2, 0, 0), ("A3L", 2, 0, 0),
    ("A3R", 2, 1, 0), ("A3L", 2, 1, 0), ("B4", 1, 0, 1), ("A2", 3, 0), ("B3", 3, 0), ("B4", 1, -1, 0),
    ("B4", 1, -1, 1), ("A4R", 0, 1, 1), ("A4L", 0, 1, 1), ("A2", 1, 1), ("B3", 2, -1), ("B4", 1, 1, 0), ("B3", 2, 1),
    ("A3R", 1, 0, 1), ("A3L", 1, 0, 1), ("A4R", 1, 1, 0), ("A4L", 1, 1, 0), ("B4", 1, 1, 1), ("B2R", 2), ("B2L", 2),
    ("C", 0, 1, 0), ("B4", 1, 2, 0), ("A4R", 2, 0, 0), ("A4L", 2, 0, 0), ("C", 0, 1, 1), ("B4", 1, 2, 1),
    ("C", 0, 1, 2), ("A4R", 2, 1, 0), ("A4L", 2, 1, 0), ("B4", 2, 2, 0), ("C", 0, 1, 3), ("A1", 2), ("C", 1, 0, 0),
    ("C", 1, 0, 1), ("A3R", 1, 1, 1), ("A3L", 1, 1, 1), ("B1R", 3), ("B1L", 3), ("C", 1, 0, 2), ("C", 1, 0, 3),
    ("A3R", 3, 0, 0), ("A3L", 3, 0, 0), ("B4", 2, 0, 0), ("B4", 2, 0, 1), ("C", 2, 0, 0), ("C", 2, 0, 1),
    ("C", 2, 0, 2), ("C", 2, 0, 3), ("A4R", 1, 0, 1), ("A4L", 1, 0, 1), ("B4", 2, -1, 0), ("B3", 3, -1),
    ("B3", 3, 1), ("B4", 2, -1, 1), ("A2", 2, 1), ("B4", 2, 1, 0), ("A3R", 2, 0, 1), ("A3L", 2, 0, 1),
    ("A4R", 1, 1, 1), ("A4L", 1, 1, 1), ("B2R", 3), ("B2L", 3), ("B4", 2, 1, 1), ("A4R", 3, 0, 0), ("A4L", 3, 0, 0),
    ("B3", 2, 2), ("A1", 3), ("A3R", 3, 1, 0), ("A3L", 3, 1, 0), ("B3", 3, 2), ("C", 1, 1, 0), ("A3R", 2, 1, 1),
    ("A3L", 2, 1, 1), ("C", 1, 1, 1), ("C", 1, 1, 2), ("B4", 3, 0, 0), ("C", 1, 1, 3), ("A4R", 2, 0, 1),
    ("A4L", 2, 0, 1), ("B4", 3, 0, 1), ("B4", 2, 2, 1), ("B4", 3, -1, 0), ("A4R", 3, 1, 0), ("A4L", 3, 1, 0),
    ("A2", 3, 1), ("A3R", 3, 0, 1), ("A3L", 3, 0, 1), ("B4", 3, -1, 1), ("A4R", 2, 1, 1), ("A4L", 2, 1, 1),
    ("B4", 3, 1, 0), ("C", 3, 0, 0), ("A3R", 3, 1, 1), ("A3L", 3, 1, 1), ("B4", 3, 1, 1), ("B4", 3, 2, 0),
    ("C", 2, 1, 0), ("A4R", 3, 0, 1), ("A4L", 3, 0, 1), ("B4", 3, 2, 1), ("C", 2, 1, 1), ("C", 2, 1, 2),
    ("C", 2, 1, 3), ("C", 3, 0, 1), ("C", 3, 0, 2), ("C", 3, 0, 3), ("A4R", 3, 1, 1), ("A4L", 3, 1, 1),
    ("C", 3, 1, 0), ("C", 3, 1, 1), ("C", 3, 1, 2), ("C", 3, 1, 3),
)
Z_FIRST = ((2, 2),)
WINDOW = {"xr": 3, "xl": 3, "y": 3, "zp": 3, "T": 2}
SEM_OF = {(0, WIDTH): 0, A_ALL: 0, A_0: 0, A_1: 1, B_ALL: 2, B_0: 2, B_1: 3}


def iota(shape, dim):
    return lax.broadcasted_iota(I32, shape, dim)


def onehot(cond):
    return cond.astype(F32).astype(BF16)


def dot(a, b, dims=((1,), (0,))):
    return lax.dot_general(a, b, (dims, ((), ())), preferred_element_type=F32)


def kernel(ids_ref, slots_ref, gates_ref, grad_hbm, hid_hbm, w_hbm, hout, wout,
           arr, outg, grad, hid, w, hmain, htail, utail, acc, sec, wbuf,
           in_sem, loc_sem, out_sem, send_sem, recv_sem, hsend_sem, hrecv_sem):
    section = lax.axis_index("section")
    z = lax.axis_index("dp")
    xy = lax.axis_index("expert")
    x, yh = lax.div(xy, 2), lax.rem(xy, 2)
    zb = lax.rem(z, 2)
    e = lax.div(z, 2)
    sg = 2 * zb - 1

    grad_in = pltpu.make_async_copy(grad_hbm, grad, in_sem.at[0])
    grad_in.start()
    hid_in = pltpu.make_async_copy(hid_hbm, hid, in_sem.at[1])
    hid_in.start()
    w_in = pltpu.make_async_copy(w_hbm, w, in_sem.at[2])
    w_in.start()

    def device(dz, dx, flip, ds=0):
        to_y = 1 - yh if flip else yh
        return (section + ds, lax.rem(z + dz + 8, 8), lax.rem(x + dx + 4, 4) * 2 + to_y)

    zflip = 1 - 2 * zb
    to_z = device(zflip, 0, False)
    to_y = device(0, 0, True)
    to_right = device(0, 1, False)
    to_left = device(0, -1, False)
    transit = {1: device(sg, 0, False), 2: device(-2 * sg, 0, False), 3: device(3 * sg, 0, False)}
    transit_from = {1: transit[1], 2: device(2 * sg, 0, False), 3: transit[3]}

    barrier = pltpu.get_barrier_semaphore()
    after = (lax.rem(section + 1, 4), z, xy)
    for other in (to_z, to_y, to_right, to_left, transit_from[1], transit_from[2], transit_from[3], after):
        pl.semaphore_signal(barrier, inc=1, device_id=other, device_id_type=MESH)

    def chunk_expert(j):
        return lax.rem(e + {0: 0, 1: sg, 2: -sg, 3: 2}[j] + 4, 4)

    experts = [chunk_expert(j) for j in range(4)]

    def expert_rows(j):
        base = jnp.full(j.shape, experts[3] * CAP, I32)
        for k in (2, 1, 0):
            base = jnp.where(j == k, experts[k] * CAP, base)
        return base

    place = ids_ref[...] * CAP + slots_ref[...]
    place0, place1 = place[0:1, :], place[1:2, :]
    gate0, gate1 = gates_ref[0:1, :], gates_ref[1:2, :]
    m = iota((128, 1), 0)
    want = expert_rows((m >> 4) & 3) + 16 * (m >> 6) + (m & 15)
    hit0, hit1 = place0 == want, place1 == want
    pick_main = onehot(hit0 | hit1)
    gate_main = jnp.sum(jnp.where(hit0, gate0, 0.0) + jnp.where(hit1, gate1, 0.0), axis=1, keepdims=True)
    m = iota((64, 1), 0)
    quarter = (m >> 2) & 3
    want = expert_rows(m >> 4) + 2 * BAND + (m & 3)
    hit0, hit1 = place0 == want, place1 == want
    tail_hit = hit0 | hit1
    gate_tail = jnp.sum(jnp.where(hit0, gate0, 0.0) + jnp.where(hit1, gate1, 0.0), axis=1, keepdims=True)

    def slot_of(j, dx=0, fy=False, fz=False):
        tz = z + zflip if fz else z
        tsg = -sg if fz else sg
        ty = 1 - yh if fy else yh
        return lax.rem(tz + tsg * j + 8, 8) * PLANE + lax.rem(x + dx + 4, 4) * 2 + ty

    mine = slot_of(0)
    grad_in.wait()
    for h in range(2):
        for c in range(0, D, 512):
            part = dot(pick_main[64 * h:64 * h + 64, :], grad[:, c:c + 512])
            part = (part * gate_main[64 * h:64 * h + 64, :]).astype(BF16)
            arr[mine, :, h * D + c:h * D + c + 512] = part[0:16]
            for j in (1, 2, 3):
                outg[j - 1, :, h * D + c:h * D + c + 512] = part[16 * j:16 * j + 16]
    part = jnp.zeros((64, QUARTER), F32)
    for q in range(4):
        part += dot(onehot(tail_hit & (quarter == q)), grad[:, q * QUARTER:(q + 1) * QUARTER])
    part = (part * gate_tail).astype(BF16)
    arr[mine, :, 2 * D:WIDTH] = part[0:16]
    for j in (1, 2, 3):
        outg[j - 1, :, 2 * D:WIDTH] = part[16 * j:16 * j + 16]

    pl.semaphore_wait(barrier, 8)

    sends = []
    lanes = {name: [] for name in WINDOW}
    seen = set()
    count = iter(range(160))

    def copy_of(place, cols, to, n):
        piece = arr.at[slot_of(*place), :, pl.ds(cols[0], cols[1])]
        return pltpu.make_async_remote_copy(
            src_ref=piece, dst_ref=piece, send_sem=send_sem.at[n],
            recv_sem=recv_sem.at[slot_of(*place), SEM_OF[cols]], device_id=to, device_id_type=MESH)

    def start(copy, lane):
        queue = lanes[lane]
        if len(queue) >= WINDOW[lane]:
            queue.pop(0).wait_send()
        copy.start()
        queue.append(copy)

    def send(place, cols, to, lane):
        start(copy_of(place, cols, to, next(count)), lane)

    def send_transit(j):
        start(pltpu.make_async_remote_copy(
            src_ref=outg.at[j - 1], dst_ref=arr.at[mine], send_sem=send_sem.at[next(count)],
            recv_sem=recv_sem.at[mine, 0], device_id=transit[j], device_id_type=MESH), "T")

    def need(j, dx=0, fy=False, fz=False, cols=None):
        dx = dx % 4
        if (dx, fy, fz) == (0, 0, 0):
            parts = [(0, WIDTH)] if j else []
        elif cols == A_ALL and dx == 2:
            parts = [A_0, A_1]
        elif cols == B_ALL and (dx, fy, fz) == (2, 0, 0):
            parts = [B_0, B_1]
        else:
            parts = [cols]
        for part in parts:
            if (j, dx, fy, fz, part) not in seen:
                seen.add((j, dx, fy, fz, part))
                copy_of((j, dx, fy, fz), part, to_z, 0).wait_recv()

    def issue(name, j=0, *rest):
        if name[0] == "T":
            send_transit(int(name[1]))
        elif name == "A1":
            need(j)
            send((j,), A_ALL, to_z, "zp")
        elif name == "A2":
            need(j, 0, False, rest[0], A_ALL)
            send((j, 0, False, rest[0]), A_ALL, to_y, "y")
        elif name in ("A3R", "A3L"):
            need(j, 0, *rest, A_ALL)
            to, lane = (to_right, "xr") if name == "A3R" else (to_left, "xl")
            send((j, 0, *rest), A_ALL, to, lane)
        elif name == "A4R":
            need(j, -1, *rest, A_ALL)
            send((j, -1, *rest), A_0, to_right, "xr")
        elif name == "A4L":
            need(j, 1, *rest, A_ALL)
            send((j, 1, *rest), A_1, to_left, "xl")
        elif name in ("B1R", "B1L"):
            need(j)
            to, lane = (to_right, "xr") if name == "B1R" else (to_left, "xl")
            send((j,), B_ALL, to, lane)
        elif name == "B2R":
            need(j, -1, False, False, B_ALL)
            send((j, -1), B_0, to_right, "xr")
        elif name == "B2L":
            need(j, 1, False, False, B_ALL)
            send((j, 1), B_1, to_left, "xl")
        else:
            dx = rest[0]
            z_first = (j, dx % 4) in Z_FIRST
            other = len(rest) > 1 and rest[1]
            place = (j, dx, False, other) if z_first else (j, dx, other, False)
            need(*place, B_ALL)
            if (name == "B3") == z_first:
                send(place, B_ALL, to_z, "zp")
            else:
                send(place, B_ALL, to_y, "y")

    def need_plane(j, fz):
        for fy in (False, True):
            for dx in range(4):
                need(j, dx, fy, fz, A_ALL)
                need(j, dx, fy, fz, B_ALL)

    v = iota((1, MAIN), 1)
    main_at = CAP * ((v >> 4) & 7) + BAND * (v >> 7) + (v & 15)
    perm_main = onehot(iota((ROWS, 1), 0) == main_at)
    u = iota((1, 128), 1)
    tail_at = CAP * ((u & 31) >> 2) + 2 * BAND + (u & 3)
    tail_match = iota((ROWS, 1), 0) == tail_at
    perm_tail = onehot(iota((ROWS, 1), 0) == tail_at)[:, 0:TAILS]

    def turn_hidden(b):
        rows = hid[ROWS * b:ROWS * b + ROWS, :]
        hmain[b] = dot(rows, perm_main, ((0,), (0,))).astype(BF16)
        spread = onehot(tail_match & ((u >> 5) == b % 4))
        part = dot(rows, spread, ((0,), (0,))).astype(BF16)
        cols = slice(128 * (b // 4), 128 * (b // 4) + 128)
        if b % 4 == 0:
            htail[:, cols] = part
        else:
            htail[:, cols] += part

    t = iota((TAILS, 1), 0)
    vt = iota((1, 128), 1)
    pick_tail = [onehot(vt == 16 * (t >> 2) + 4 * q + (t & 3)) for q in range(4)]

    def unpack_tails(b):
        packed = arr[pl.ds(PLANE * b, PLANE), :, 2 * D:WIDTH].reshape(PLANE * BAND, QUARTER)
        at = pl.multiple_of(b * TAILS, TAILS)
        for q in range(4):
            utail[pl.ds(at, TAILS), q * QUARTER:(q + 1) * QUARTER] = dot(pick_tail[q], packed).astype(BF16)

    def band(b, h, c, n):
        return arr[pl.ds(PLANE * b, PLANE), :, h * D + c:h * D + c + n].reshape(PLANE * BAND, n)

    def hidden_copy(b):
        rows = pl.ds(pl.multiple_of(b * ROWS, ROWS), ROWS)
        return pltpu.make_async_remote_copy(
            src_ref=sec.at[rows], dst_ref=hout.at[rows], send_sem=hsend_sem.at[b],
            recv_sem=hrecv_sem.at[b], device_id=device(0, 0, False, -1), device_id_type=MESH)

    def section_part(b):
        at = pl.multiple_of(b * TAILS, TAILS)
        out = jnp.zeros((MAIN + TAILS, UNITS), F32)
        for c in range(0, D, SECTION_STEP):
            rows = jnp.concatenate(
                [band(b, 0, c, SECTION_STEP), band(b, 1, c, SECTION_STEP),
                 utail[pl.ds(at, TAILS), c:c + SECTION_STEP]], axis=0)
            out += dot(rows, w[:, c:c + SECTION_STEP], ((1,), (1,)))
        out = out.astype(BF16)
        out = dot(perm_main, out[0:MAIN]) + dot(perm_tail, out[MAIN:])
        sec[pl.ds(pl.multiple_of(b * ROWS, ROWS), ROWS), :] = out.astype(BF16)
        hidden_copy(b).start()

    def weight_part(b, c, n, first, last):
        rows = jnp.concatenate([band(b, 0, c, n), band(b, 1, c, n)], axis=0)
        part = dot(hmain[b], rows)
        if not first:
            part += acc[:, c:c + n]
        if not last:
            acc[:, c:c + n] = part
        else:
            part += dot(htail[...], utail[:, c:c + n])
            wbuf[:, c:c + n] = part.astype(BF16)
            pltpu.make_async_copy(wbuf.at[:, c:c + n], wout.at[:, c:c + n], out_sem.at[c // n]).start()

    def compute(j, fz, piece):
        fz = bool(fz)
        b = lax.div(slot_of(j, 0, False, fz), PLANE)
        if piece == 0:
            need_plane(j, fz)
            unpack_tails(b)

            @pl.when(section > 0)
            def _():
                section_part(b)
        else:
            for c in (0, 512):
                at = (piece - 1) * 1024 + c
                weight_part(b, at, 512, (j, fz) == planes[0], (j, fz) == planes[-1])

    planes = [(step[1], bool(step[2])) for step in ORDER if step[0] == "C" and step[3] == 0]
    for step in ORDER:
        if step[0] == "H":
            if step[1] == 0:
                hid_in.wait()
            turn_hidden(step[1])
        elif step[0] == "C":
            if step[1:3] == planes[0] and step[3] == 0:
                w_in.wait()
            compute(*step[1:])
        else:
            issue(*step)
    for queue in lanes.values():
        sends.extend(queue)

    @pl.when(section == 3)
    def _():
        hid[...] = jnp.zeros((SLOTS, UNITS), BF16)
        zero = pltpu.make_async_copy(hid, hout, loc_sem)
        zero.start()
        zero.wait()

    for c in range(0, D, 512):
        pltpu.make_async_copy(wbuf.at[:, c:c + 512], wout.at[:, c:c + 512], out_sem.at[c // 512]).wait()
    for copy in sends:
        copy.wait_send()

    @pl.when(section > 0)
    def _():
        for b in range(BLOCKS):
            hidden_copy(b).wait_send()

    @pl.when(section < 3)
    def _():
        for b in range(BLOCKS):
            hidden_copy(b).wait_recv()


def body(grad_out, expert_ids, slot_ids, gates, hidden, w_down):
    anywhere = pl.BlockSpec(memory_space=pl.ANY)
    vmem = pl.BlockSpec(memory_space=pltpu.VMEM)
    dma = pltpu.SemaphoreType.DMA
    hout, wout = pl.pallas_call(
        kernel,
        out_shape=(jax.ShapeDtypeStruct((SLOTS, UNITS), BF16), jax.ShapeDtypeStruct((UNITS, D), BF16)),
        in_specs=[vmem] * 3 + [anywhere] * 3,
        out_specs=(anywhere, anywhere),
        scratch_shapes=[
            pltpu.VMEM((BLOCKS * PLANE, BAND, WIDTH), BF16),
            pltpu.VMEM((3, BAND, WIDTH), BF16),
            pltpu.VMEM((128, D), BF16),
            pltpu.VMEM((SLOTS, UNITS), BF16),
            pltpu.VMEM((UNITS, D), BF16),
            pltpu.VMEM((BLOCKS, UNITS, MAIN), BF16),
            pltpu.VMEM((UNITS, BLOCKS * TAILS), BF16),
            pltpu.VMEM((BLOCKS * TAILS, D), BF16),
            pltpu.VMEM((UNITS, D), F32),
            pltpu.VMEM((SLOTS, UNITS), BF16),
            pltpu.VMEM((UNITS, D), BF16),
            dma((3,)), dma, dma((6,)), dma((160,)), dma((64, 4)), dma((8,)), dma((8,)),
        ],
        compiler_params=pltpu.CompilerParams(
            collective_id=0, has_side_effects=True, vmem_limit_bytes=56 * 2**20),
        cost_estimate=pl.CostEstimate(flops=15 * 10**9, bytes_accessed=12 * 10**6, transcendentals=0),
        name="dispatch_and_products",
    )(expert_ids[0].T, slot_ids[0].T, gates[0].T, grad_out[0], hidden[0], w_down[0])
    return (hout[None], wout[None])


def solution(mesh):
    in_specs = (
        P("section", ("dp", "expert"), None),
        P("section", ("dp", "expert"), None),
        P("section", ("dp", "expert"), None),
        P("section", ("dp", "expert"), None),
        P("section", None, ("dp", "expert")),
        P("section", ("dp", "expert"), None),
    )
    out_specs = (P("section", None, ("dp", "expert")), P("section", ("dp", "expert"), None))
    return jax.shard_map(body, mesh=mesh, in_specs=in_specs, out_specs=out_specs, check_vma=False)
```

```python
import functools

import jax
import jax.numpy as jnp
from jax import lax
from jax.experimental import pallas as pl
from jax.experimental.pallas import tpu as pltpu
from jax.sharding import PartitionSpec as P

MESH = pl.DeviceIdType.MESH
FLIGHT = 4
BF16, F32, I32 = jnp.bfloat16, jnp.float32, jnp.int32

D = 3072
CAP = 36
BAND = 16
TAIL = CAP - 2 * BAND
QUARTER = D // 4
WIDTH = 2 * D + QUARTER
UNITS = 512
BLOCKS = 8
PLANE = 8
ROWS = PLANE * CAP
SLOTS = BLOCKS * ROWS
MAIN = PLANE * 2 * BAND
TAILS = PLANE * TAIL
SECTION_STEP = 768
HALF_A = 16 * 128
HALF_B = (WIDTH - 2 * HALF_A) // 2
A_ALL = (0, 2 * HALF_A)
A_0 = (0, HALF_A)
A_1 = (HALF_A, HALF_A)
B_ALL = (2 * HALF_A, 2 * HALF_B)
B_0 = (2 * HALF_A, HALF_B)
B_1 = (2 * HALF_A + HALF_B, HALF_B)
ORDER = (
    ("A2", 0, 0), ("A1", 0), ("B1R", 0), ("B1L", 0), ("B3", 0, 0), ("A3R", 0, 0, 0), ("A3L", 0, 0, 0),
    ("B4", 0, 0, 0), ("H", 0), ("T1",), ("H", 1), ("H", 2), ("H", 3), ("H", 4), ("H", 5), ("H", 6), ("H", 7),
    ("B3", 0, -1), ("B3", 0, 1), ("B2R", 0), ("B2L", 0), ("B4", 0, -1, 0), ("B4", 0, 0, 1), ("A3R", 0, 1, 0),
    ("A2", 0, 1), ("T2",), ("A3L", 0, 0, 1), ("A3R", 0, 0, 1), ("A3L", 0, 1, 0), ("B3", 0, 2), ("A2", 1, 0),
    ("A1", 1), ("B4", 0, 1, 0), ("B1R", 1), ("B1L", 1), ("A4R", 0, 0, 0), ("A4L", 0, 0, 0), ("B3", 1, 0),
    ("A4R", 0, 0, 1), ("A4L", 0, 0, 1), ("A4R", 0, 1, 0), ("A4L", 0, 1, 0), ("B3", 1, -1), ("B4", 0, -1, 1),
    ("B2R", 1), ("B2L", 1), ("A3R", 0, 1, 1), ("A3L", 0, 1, 1), ("B3", 1, 1), ("B4", 0, 1, 1), ("A3R", 1, 0, 0),
    ("A3L", 1, 0, 0), ("C", 0, 0, 0), ("T3",), ("A2", 1, 1), ("C", 0, 0, 1), ("B3", 1, 2), ("C", 0, 0, 2), ("A1", 2),
    ("C", 0, 0, 3), ("A2", 2, 0), ("B1R", 2), ("B1L", 2), ("B4", 0, 2, 0), ("A4R", 0, 1, 1), ("A4L", 0, 1, 1),
    ("A3R", 1, 0, 1), ("B3", 2, 0), ("A3L", 1, 0, 1), ("A3R", 1, 1, 0), ("A3L", 1, 1, 0), ("B3", 2, -1),
    ("B4", 0, 2, 1), ("B4", 1, 0, 0), ("A2", 2, 1), ("B2R", 2), ("B2L", 2), ("A3R", 1, 1, 1), ("B3", 2, 1),
    ("A3L", 1, 1, 1), ("A4R", 1, 0, 0), ("A4L", 1, 0, 0), ("B4", 1, 0, 1), ("B4", 1, -1, 0), ("B3", 2, 2),
    ("C", 0, 1, 0), ("B1R", 3), ("B1L", 3), ("C", 0, 1, 1), ("A4R", 1, 0, 1), ("A4L", 1, 0, 1), ("A2", 3, 0),
    ("C", 0, 1, 2), ("A1", 3), ("C", 0, 1, 3), ("B3", 3, 0), ("B4", 1, -1, 1), ("A4R", 1, 1, 0), ("A4L", 1, 1, 0),
    ("A4R", 1, 1, 1), ("A4L", 1, 1, 1), ("B3", 3, -1), ("B4", 1, 1, 0), ("B2R", 3), ("B2L", 3), ("A3R", 2, 0, 0),
    ("B4", 1, 1, 1), ("A3L", 2, 0, 0), ("B3", 3, 1), ("C", 1, 0, 0), ("A3R", 2, 0, 1), ("A2", 3, 1),
    ("A3L", 2, 0, 1), ("C", 1, 0, 1), ("B4", 1, 2, 0), ("C", 1, 0, 2), ("C", 1, 0, 3), ("B4", 1, 2, 1), ("B3", 3, 2),
    ("A3R", 2, 1, 0), ("A3L", 2, 1, 0), ("B4", 2, 0, 0), ("B4", 2, 0, 1), ("A3R", 2, 1, 1), ("A3L", 2, 1, 1),
    ("C", 1, 1, 0), ("A4R", 2, 0, 0), ("A4L", 2, 0, 0), ("B4", 2, -1, 0), ("C", 1, 1, 1), ("C", 1, 1, 2),
    ("C", 1, 1, 3), ("B4", 2, -1, 1), ("A4R", 2, 0, 1), ("A4L", 2, 0, 1), ("A4R", 2, 1, 0), ("A4L", 2, 1, 0),
    ("B4", 2, 1, 0), ("B4", 2, 1, 1), ("A4R", 2, 1, 1), ("A4L", 2, 1, 1), ("A3R", 3, 0, 0), ("A3L", 3, 0, 0),
    ("C", 2, 0, 0), ("B4", 2, 2, 0), ("B4", 2, 2, 1), ("A3R", 3, 0, 1), ("A3L", 3, 0, 1), ("C", 2, 0, 1),
    ("C", 2, 0, 2), ("C", 2, 0, 3), ("A3R", 3, 1, 0), ("A3L", 3, 1, 0), ("B4", 3, 0, 0), ("B4", 3, 0, 1),
    ("C", 2, 1, 0), ("A3R", 3, 1, 1), ("A3L", 3, 1, 1), ("C", 2, 1, 1), ("C", 2, 1, 2), ("A4R", 3, 0, 0),
    ("A4L", 3, 0, 0), ("B4", 3, -1, 0), ("B4", 3, -1, 1), ("C", 2, 1, 3), ("C", 3, 0, 0), ("A4R", 3, 0, 1),
    ("A4L", 3, 0, 1), ("B4", 3, 1, 0), ("B4", 3, 1, 1), ("A4R", 3, 1, 0), ("A4L", 3, 1, 0), ("A4R", 3, 1, 1),
    ("A4L", 3, 1, 1), ("B4", 3, 2, 0), ("B4", 3, 2, 1), ("C", 3, 0, 1), ("C", 3, 0, 2), ("C", 3, 0, 3),
    ("C", 3, 0, 4), ("C", 3, 1, 0), ("C", 3, 1, 1), ("C", 3, 1, 2), ("C", 3, 1, 3), ("C", 3, 1, 4),
)
SPLIT = ((3, False), (3, True))
Y_FIRST = ()
Z_FIRST = ()
WINDOW = {"xr": 8, "xl": 8, "y": 8, "zp": 8, "T": 8}
SEM_OF = {(0, WIDTH): 0, A_ALL: 0, A_0: 0, A_1: 1, B_ALL: 2, B_0: 2, B_1: 3}


def iota(shape, dim):
    return lax.broadcasted_iota(I32, shape, dim)


def onehot(cond):
    return cond.astype(F32).astype(BF16)


def dot(a, b, dims=((1,), (0,))):
    return lax.dot_general(a, b, (dims, ((), ())), preferred_element_type=F32)


def kernel(ids_ref, slots_ref, gates_ref, grad_hbm, hid_hbm, w_hbm, hout, wout,
           arr, outg, grad, hid, w, hmain, htail, utail, acc, sec,
           in_sem, send_sem, recv_sem, hsend_sem, hrecv_sem):
    section = lax.axis_index("section")
    z = lax.axis_index("dp")
    xy = lax.axis_index("expert")
    x, yh = lax.div(xy, 2), lax.rem(xy, 2)
    zb = lax.rem(z, 2)
    e = lax.div(z, 2)
    sg = 2 * zb - 1

    grad_in = pltpu.make_async_copy(grad_hbm, grad, in_sem.at[0])
    grad_in.start()
    hid_in = pltpu.make_async_copy(hid_hbm, hid, in_sem.at[1])
    hid_in.start()
    w_in = pltpu.make_async_copy(w_hbm, w, in_sem.at[2])
    w_in.start()

    def device(dz, dx, flip, ds=0):
        to_y = 1 - yh if flip else yh
        return (section + ds, lax.rem(z + dz + 8, 8), lax.rem(x + dx + 4, 4) * 2 + to_y)

    zflip = 1 - 2 * zb
    to_z = device(zflip, 0, False)
    to_y = device(0, 0, True)
    to_right = device(0, 1, False)
    to_left = device(0, -1, False)
    transit = {1: device(sg, 0, False), 2: device(-2 * sg, 0, False), 3: device(3 * sg, 0, False)}
    transit_from = {1: transit[1], 2: device(2 * sg, 0, False), 3: transit[3]}

    barrier = pltpu.get_barrier_semaphore()
    after = (lax.rem(section + 1, 4), z, xy)
    for other in (to_z, to_y, to_right, to_left, transit_from[1], transit_from[2], transit_from[3], after):
        pl.semaphore_signal(barrier, inc=1, device_id=other, device_id_type=MESH)

    def chunk_expert(j):
        return lax.rem(e + {0: 0, 1: sg, 2: -sg, 3: 2}[j] + 4, 4)

    experts = [chunk_expert(j) for j in range(4)]

    def expert_rows(j):
        base = jnp.full(j.shape, experts[3] * CAP, I32)
        for k in (2, 1, 0):
            base = jnp.where(j == k, experts[k] * CAP, base)
        return base

    def slot_of(j, dx=0, fy=False, fz=False):
        tz = z + zflip if fz else z
        tsg = -sg if fz else sg
        ty = 1 - yh if fy else yh
        return lax.rem(tz + tsg * j + 8, 8) * PLANE + lax.rem(x + dx + 4, 4) * 2 + ty

    place = ids_ref[...] * CAP + slots_ref[...]
    place0, place1 = place[0:1, :], place[1:2, :]
    gate0, gate1 = gates_ref[0:1, :], gates_ref[1:2, :]
    mine = slot_of(0)

    def match(want):
        hit0, hit1 = place0 == want, place1 == want
        gate = jnp.sum(jnp.where(hit0, gate0, 0.0) + jnp.where(hit1, gate1, 0.0), axis=1, keepdims=True)
        return hit0 | hit1, gate

    def pack(rounds):
        n = len(rounds)
        targets = [arr.at[mine] if j == 0 else outg.at[j - 1] for j in rounds]
        m = iota((BAND * n, 1), 0)
        base = expert_rows((m >> 4) + rounds[0])
        for h in range(2):
            hit, gate = match(base + BAND * h + (m & 15))
            pick = onehot(hit)
            for c in range(0, D, 512):
                part = (dot(pick, grad[:, c:c + 512]) * gate).astype(BF16)
                for k in range(n):
                    targets[k][:, h * D + c:h * D + c + 512] = part[BAND * k:BAND * (k + 1)]
        hit, gate = match(base + 2 * BAND + (m & 3))
        part = jnp.zeros((BAND * n, QUARTER), F32)
        for q in range(4):
            part += dot(onehot(hit & (((m >> 2) & 3) == q)), grad[:, q * QUARTER:(q + 1) * QUARTER])
        part = (part * gate).astype(BF16)
        for k in range(n):
            targets[k][:, 2 * D:WIDTH] = part[BAND * k:BAND * (k + 1)]

    grad_in.wait()
    pack((0,))
    pl.semaphore_wait(barrier, 8)

    sends = []
    lanes = {name: [] for name in WINDOW}
    seen = set()
    count = iter(range(160))

    def copy_of(place, cols, to, n):
        piece = arr.at[slot_of(*place), :, pl.ds(cols[0], cols[1])]
        return pltpu.make_async_remote_copy(
            src_ref=piece, dst_ref=piece, send_sem=send_sem.at[n],
            recv_sem=recv_sem.at[slot_of(*place), SEM_OF[cols]], device_id=to, device_id_type=MESH)

    def start(copy, lane):
        queue = lanes[lane]
        if len(queue) >= WINDOW[lane]:
            queue.pop(0).wait_send()
        copy.start()
        queue.append(copy)

    def send(place, cols, to, lane):
        start(copy_of(place, cols, to, next(count)), lane)

    def send_transit(j):
        start(pltpu.make_async_remote_copy(
            src_ref=outg.at[j - 1], dst_ref=arr.at[mine], send_sem=send_sem.at[next(count)],
            recv_sem=recv_sem.at[mine, 0], device_id=transit[j], device_id_type=MESH), "T")

    def need(j, dx=0, fy=False, fz=False, cols=None):
        dx = dx % 4
        if (dx, fy, fz) == (0, 0, 0):
            parts = [(0, WIDTH)] if j else []
        elif cols == A_ALL and dx == 2:
            parts = [A_0, A_1]
        elif cols == B_ALL and (dx, fy, fz) == (2, 0, 0):
            parts = [B_0, B_1]
        else:
            parts = [cols]
        for part in parts:
            if (j, dx, fy, fz, part) not in seen:
                seen.add((j, dx, fy, fz, part))
                copy_of((j, dx, fy, fz), part, to_z, 0).wait_recv()

    def issue(name, j=0, *rest):
        if name[0] == "T":
            send_transit(int(name[1]))
        elif name == "A1":
            need(j)
            if j in Y_FIRST:
                send((j,), A_ALL, to_y, "y")
            else:
                send((j,), A_ALL, to_z, "zp")
        elif name == "A2" and j in Y_FIRST:
            need(j, 0, rest[0], False, A_ALL)
            send((j, 0, rest[0], False), A_ALL, to_z, "zp")
        elif name == "A2":
            need(j, 0, False, rest[0], A_ALL)
            send((j, 0, False, rest[0]), A_ALL, to_y, "y")
        elif name in ("A3R", "A3L"):
            need(j, 0, *rest, A_ALL)
            to, lane = (to_right, "xr") if name == "A3R" else (to_left, "xl")
            send((j, 0, *rest), A_ALL, to, lane)
        elif name == "A4R":
            need(j, -1, *rest, A_ALL)
            send((j, -1, *rest), A_0, to_right, "xr")
        elif name == "A4L":
            need(j, 1, *rest, A_ALL)
            send((j, 1, *rest), A_1, to_left, "xl")
        elif name in ("B1R", "B1L"):
            need(j)
            to, lane = (to_right, "xr") if name == "B1R" else (to_left, "xl")
            send((j,), B_ALL, to, lane)
        elif name == "B2R":
            need(j, -1, False, False, B_ALL)
            send((j, -1), B_0, to_right, "xr")
        elif name == "B2L":
            need(j, 1, False, False, B_ALL)
            send((j, 1), B_1, to_left, "xl")
        else:
            dx = rest[0]
            z_first = (j, dx % 4) in Z_FIRST
            other = len(rest) > 1 and rest[1]
            place = (j, dx, False, other) if z_first else (j, dx, other, False)
            need(*place, B_ALL)
            if (name == "B3") == z_first:
                send(place, B_ALL, to_z, "zp")
            else:
                send(place, B_ALL, to_y, "y")

    def need_plane(j, fz, far):
        for fy in (False, True):
            for dx in (0, 1, 3, 2) if far else (0, 1, 3):
                need(j, dx, fy, fz, A_ALL)
                need(j, dx, fy, fz, B_ALL)

    v = iota((1, MAIN), 1)
    main_at = CAP * ((v >> 4) & 7) + BAND * (v >> 7) + (v & 15)
    perm_main = onehot(iota((ROWS, 1), 0) == main_at)
    u = iota((1, 128), 1)
    tail_at = CAP * ((u & 31) >> 2) + 2 * BAND + (u & 3)
    tail_match = iota((ROWS, 1), 0) == tail_at
    perm_tail = onehot(iota((ROWS, 1), 0) == tail_at)[:, 0:TAILS]

    def turn_hidden(b):
        rows = hid[ROWS * b:ROWS * b + ROWS, :]
        hmain[b] = dot(rows, perm_main, ((0,), (0,))).astype(BF16)
        spread = onehot(tail_match & ((u >> 5) == b % 4))
        part = dot(rows, spread, ((0,), (0,))).astype(BF16)
        cols = slice(128 * (b // 4), 128 * (b // 4) + 128)
        if b % 4 == 0:
            htail[:, cols] = part
        else:
            htail[:, cols] += part

    def perms(sources):
        at = iota((sources * CAP, 1), 0)
        p = iota((1, sources * 2 * BAND), 1)
        main = onehot(at == CAP * ((p >> 4) & (sources - 1)) + BAND * (p >> (4 + sources.bit_length() - 1)) + (p & 15))
        q = iota((1, 128), 1)
        tail = onehot(at == CAP * (q >> 2) + 2 * BAND + (q & 3))[:, 0:sources * TAIL]
        return main, tail

    perms_whole, perms_half = perms(PLANE), perms(PLANE // 2)

    def unpack_tails(start, sources):
        packed = arr[pl.ds(start, sources), :, 2 * D:WIDTH].reshape(sources * BAND, QUARTER)
        t = iota((sources * TAIL, 1), 0)
        v = iota((1, sources * BAND), 1)
        rows = pl.ds(pl.multiple_of(start * TAIL, BAND), sources * TAIL)
        for q in range(4):
            pick = onehot(v == BAND * (t >> 2) + 4 * q + (t & 3))
            utail[rows, q * QUARTER:(q + 1) * QUARTER] = dot(pick, packed).astype(BF16)

    def band(b, h, c, n):
        return arr[pl.ds(PLANE * b, PLANE), :, h * D + c:h * D + c + n].reshape(PLANE * BAND, n)

    def hidden_copy(b, side, at, rows):
        piece = pl.ds(pl.multiple_of(at, BAND), rows)
        return pltpu.make_async_remote_copy(
            src_ref=sec.at[piece], dst_ref=hout.at[piece], send_sem=hsend_sem.at[b, side],
            recv_sem=hrecv_sem.at[b, side], device_id=device(0, 0, False, -1), device_id_type=MESH)

    def pair_of(side):
        near = lax.div(x, 2)
        return 1 - near if side else near

    def plane_at(plane):
        return lax.div(slot_of(plane[0], 0, False, plane[1]), PLANE)

    def hidden_copies(plane, sides=(0, 1)):
        b = plane_at(plane)
        if plane in SPLIT:
            return [hidden_copy(b, side, b * ROWS + pair_of(side) * (ROWS // 2), ROWS // 2) for side in sides]
        return [hidden_copy(b, 0, b * ROWS, ROWS)]

    def section_part(b, start, sources, perms):
        mains, tails = sources * 2 * BAND, sources * TAIL
        rows = jnp.concatenate(
            [arr[pl.ds(start, sources), :, 0:D].reshape(mains // 2, D),
             arr[pl.ds(start, sources), :, D:2 * D].reshape(mains // 2, D),
             utail[pl.ds(pl.multiple_of(start * TAIL, BAND), tails), :]], axis=0)
        out = dot(rows, w[...], ((1,), (1,))).astype(BF16)
        out = dot(perms[0], out[0:mains]) + dot(perms[1], out[mains:])
        sec[pl.ds(pl.multiple_of(start * CAP, BAND), sources * CAP), :] = out.astype(BF16)

    def weight_part(b, c, n, first, last):
        rows = jnp.concatenate([band(b, 0, c, n), band(b, 1, c, n)], axis=0)
        part = dot(hmain[b], rows)
        if not first:
            part += acc[:, c:c + n]
        if not last:
            acc[:, c:c + n] = part
        else:
            part += dot(htail[...], utail[:, c:c + n])
            wout[:, c:c + n] = part.astype(BF16)

    def compute(j, fz, piece):
        plane = (j, bool(fz))
        b = plane_at(plane)
        sections = 2 if plane in SPLIT else 1
        if piece < sections:
            need_plane(*plane, far=piece == sections - 1)
            start = b * PLANE
            if sections == 2:
                start = start + pair_of(piece) * (PLANE // 2)
            unpack_tails(start, PLANE // sections)

            @pl.when(section > 0)
            def _():
                section_part(b, start, PLANE // sections, perms_half if sections == 2 else perms_whole)
                hidden_copies(plane, (piece,))[0].start()
        else:
            for c in (0, 512):
                at = (piece - sections) * 1024 + c
                weight_part(b, at, 512, plane == planes[0], plane == planes[-1])

    planes = [(step[1], bool(step[2])) for step in ORDER if step[0] == "C" and step[3] == 0]
    for step in ORDER:
        if step[0] == "H":
            if step[1] == 0:
                hid_in.wait()
            turn_hidden(step[1])
        elif step[0] == "C":
            if step[1:3] == planes[0] and step[3] == 0:
                w_in.wait()
            compute(*step[1:])
        else:
            if step == ("T1",):
                pack((1, 2, 3))
            issue(*step)
    for queue in lanes.values():
        sends.extend(queue)

    @pl.when(section == 3)
    def _():
        hout[...] = jnp.zeros((SLOTS, UNITS), BF16)

    for copy in sends:
        copy.wait_send()

    @pl.when(section > 0)
    def _():
        for plane in planes:
            for copy in hidden_copies(plane):
                copy.wait_send()

    @pl.when(section < 3)
    def _():
        for plane in planes:
            for copy in hidden_copies(plane):
                copy.wait_recv()


def body(grad_out, expert_ids, slot_ids, gates, hidden, w_down):
    anywhere = pl.BlockSpec(memory_space=pl.ANY)
    vmem = pl.BlockSpec(memory_space=pltpu.VMEM)
    dma = pltpu.SemaphoreType.DMA
    hout, wout = pl.pallas_call(
        kernel,
        out_shape=(pltpu.VMEM((SLOTS, UNITS), BF16), pltpu.VMEM((UNITS, D), BF16)),
        in_specs=[vmem] * 3 + [anywhere] * 3,
        out_specs=(vmem, vmem),
        scratch_shapes=[
            pltpu.VMEM((BLOCKS * PLANE, BAND, WIDTH), BF16),
            pltpu.VMEM((3, BAND, WIDTH), BF16),
            pltpu.VMEM((128, D), BF16),
            pltpu.VMEM((SLOTS, UNITS), BF16),
            pltpu.VMEM((UNITS, D), BF16),
            pltpu.VMEM((BLOCKS, UNITS, MAIN), BF16),
            pltpu.VMEM((UNITS, BLOCKS * TAILS), BF16),
            pltpu.VMEM((BLOCKS * TAILS, D), BF16),
            pltpu.VMEM((UNITS, D), F32),
            pltpu.VMEM((SLOTS, UNITS), BF16),
            dma((3,)), dma((160,)), dma((64, 4)), dma((8, 2)), dma((8, 2)),
        ],
        compiler_params=pltpu.CompilerParams(
            collective_id=0, has_side_effects=True, vmem_limit_bytes=54 * 2**20),
        cost_estimate=pl.CostEstimate(flops=15 * 10**9, bytes_accessed=12 * 10**6, transcendentals=0),
        name="dispatch_and_products",
    )(expert_ids[0].T, slot_ids[0].T, gates[0].T, grad_out[0], hidden[0], w_down[0])
    return (hout[None], wout[None])


def solution(mesh):
    in_specs = (
        P("section", ("dp", "expert"), None),
        P("section", ("dp", "expert"), None),
        P("section", ("dp", "expert"), None),
        P("section", ("dp", "expert"), None),
        P("section", None, ("dp", "expert")),
        P("section", ("dp", "expert"), None),
    )
    out_specs = (P("section", None, ("dp", "expert")), P("section", ("dp", "expert"), None))
    return jax.shard_map(body, mesh=mesh, in_specs=in_specs, out_specs=out_specs, check_vma=False)
```

```python
import functools

import jax
import jax.numpy as jnp
from jax import lax
from jax.experimental import pallas as pl
from jax.experimental.pallas import tpu as pltpu
from jax.sharding import PartitionSpec as P

MESH = pl.DeviceIdType.MESH
FLIGHT = 4
BF16, F32, I32 = jnp.bfloat16, jnp.float32, jnp.int32

D = 3072
CAP = 36
BAND = 16
TAIL = CAP - 2 * BAND
QUARTER = D // 4
WIDTH = 2 * D + QUARTER
UNITS = 512
BLOCKS = 8
PLANE = 8
ROWS = PLANE * CAP
SLOTS = BLOCKS * ROWS
MAIN = PLANE * 2 * BAND
TAILS = PLANE * TAIL
SECTION_STEP = 768
HALF_A = 16 * 128
HALF_B = (WIDTH - 2 * HALF_A) // 2
A_ALL = (0, 2 * HALF_A)
A_0 = (0, HALF_A)
A_1 = (HALF_A, HALF_A)
B_ALL = (2 * HALF_A, 2 * HALF_B)
B_0 = (2 * HALF_A, HALF_B)
B_1 = (2 * HALF_A + HALF_B, HALF_B)
ORDER = (
    ("A1", 0), ("A2", 0, 0), ("B1R", 0), ("B1L", 0), ("B3", 0, 0), ("A3R", 0, 0, 0), ("A3L", 0, 0, 0),
    ("B4", 0, 0, 0), ("H", 0), ("T1",), ("T2",), ("T3",), ("H", 1), ("H", 2), ("H", 3), ("H", 4), ("H", 5), ("H", 6),
    ("H", 7), ("B3", 0, -1), ("B3", 0, 1), ("B2R", 0), ("B2L", 0), ("A3R", 0, 1, 0), ("A3L", 0, 1, 0),
    ("A4R", 0, 0, 0), ("A4L", 0, 0, 0), ("B3", 0, 2), ("B4", 0, 0, 1), ("B4", 0, -1, 0), ("A2", 0, 1),
    ("A3R", 0, 0, 1), ("A3L", 0, 0, 1), ("A4R", 0, 1, 0), ("A4L", 0, 1, 0), ("A3R", 0, 1, 1), ("A3L", 0, 1, 1),
    ("A4R", 0, 0, 1), ("A4L", 0, 0, 1), ("B4", 0, -1, 1), ("C", 0, 0, 0), ("B4", 0, 1, 0), ("C", 0, 0, 1),
    ("C", 0, 0, 2), ("C", 0, 0, 3), ("A4R", 0, 1, 1), ("A4L", 0, 1, 1), ("A2", 1, 0), ("B1R", 1), ("B1L", 1),
    ("B3", 1, 0), ("A3R", 1, 0, 0), ("A2", 2, 0), ("A1", 1), ("B1L", 2), ("B1R", 2), ("A3L", 1, 0, 0), ("A1", 2),
    ("B1L", 3), ("B1R", 3), ("B3", 2, 0), ("B4", 0, 1, 1), ("A3L", 2, 0, 0), ("B2R", 1), ("B4", 0, 2, 0),
    ("A2", 1, 1), ("A3R", 1, 0, 1), ("B3", 1, -1), ("B2L", 1), ("B4", 0, 2, 1), ("A3R", 1, 1, 0), ("A1", 3),
    ("A3L", 1, 0, 1), ("B2R", 2), ("B3", 1, 1), ("A3L", 1, 1, 0), ("B4", 1, 0, 0), ("A4R", 1, 0, 0), ("B3", 1, 2),
    ("B2L", 2), ("C", 0, 1, 0), ("A2", 2, 1), ("B4", 1, 0, 1), ("C", 0, 1, 1), ("A3R", 2, 0, 0), ("C", 0, 1, 2),
    ("B3", 2, -1), ("C", 0, 1, 3), ("A3L", 1, 1, 1), ("B4", 1, -1, 0), ("A3R", 1, 1, 1), ("A4R", 1, 0, 1),
    ("A4L", 1, 0, 0), ("B4", 1, -1, 1), ("B3", 2, 1), ("A4L", 1, 0, 1), ("B4", 1, 1, 0), ("A4R", 1, 1, 0),
    ("B3", 2, 2), ("A4L", 1, 1, 0), ("B4", 1, 1, 1), ("A2", 3, 0), ("A3L", 2, 0, 1), ("A3R", 2, 0, 1),
    ("B4", 1, 2, 0), ("A2", 3, 1), ("A3L", 2, 1, 0), ("A3R", 2, 1, 0), ("A3R", 2, 1, 1), ("B4", 1, 2, 1),
    ("A4L", 1, 1, 1), ("C", 1, 0, 0), ("B3", 3, 0), ("B4", 2, 0, 0), ("B4", 2, 0, 1), ("C", 1, 0, 1), ("C", 1, 0, 2),
    ("C", 1, 0, 3), ("A3L", 2, 1, 1), ("B3", 3, -1), ("B2L", 3), ("A4R", 1, 1, 1), ("B3", 3, 1), ("B4", 2, -1, 0),
    ("B4", 2, -1, 1), ("A4L", 2, 0, 0), ("B2R", 3), ("A4R", 2, 0, 0), ("A4L", 2, 0, 1), ("A4R", 2, 0, 1),
    ("A4R", 2, 1, 0), ("B4", 2, 1, 0), ("B4", 2, 1, 1), ("A4L", 2, 1, 0), ("C", 1, 1, 0), ("B3", 3, 2),
    ("A4R", 2, 1, 1), ("A3L", 3, 0, 0), ("A3L", 3, 0, 1), ("C", 1, 1, 1), ("C", 1, 1, 2), ("A3R", 3, 0, 0),
    ("A3R", 3, 0, 1), ("C", 1, 1, 3), ("B4", 2, 2, 0), ("B4", 2, 2, 1), ("A4L", 2, 1, 1), ("C", 2, 0, 0),
    ("A3R", 3, 1, 0), ("C", 2, 0, 1), ("C", 2, 0, 2), ("C", 2, 0, 3), ("B4", 3, 0, 0), ("B4", 3, 0, 1),
    ("A3L", 3, 1, 0), ("C", 2, 1, 0), ("A3L", 3, 1, 1), ("A3R", 3, 1, 1), ("A4L", 3, 0, 0), ("B4", 3, -1, 0),
    ("B4", 3, -1, 1), ("A4R", 3, 0, 0), ("A4R", 3, 0, 1), ("A4L", 3, 0, 1), ("B4", 3, 1, 0), ("B4", 3, 1, 1),
    ("A4R", 3, 1, 0), ("A4L", 3, 1, 0), ("C", 3, 0, 0), ("A4L", 3, 1, 1), ("B4", 3, 2, 0), ("B4", 3, 2, 1),
    ("A4R", 3, 1, 1), ("C", 3, 0, 1), ("C", 3, 1, 0), ("C", 3, 1, 1), ("C", 2, 1, 1), ("C", 2, 1, 2), ("C", 2, 1, 3),
    ("C", 3, 0, 2), ("C", 3, 0, 3), ("C", 3, 0, 4), ("C", 3, 1, 2), ("C", 3, 1, 3), ("C", 3, 1, 4),
)
SPLIT = ((3, False), (3, True))
Y_FIRST = ()
Z_FIRST = ()
WINDOW = {"xr": 8, "xl": 8, "y": 8, "zp": 8, "T": 8}
SEM_OF = {(0, WIDTH): 0, A_ALL: 0, A_0: 0, A_1: 1, B_ALL: 2, B_0: 2, B_1: 3}


def iota(shape, dim):
    return lax.broadcasted_iota(I32, shape, dim)


def onehot(cond):
    return cond.astype(F32).astype(BF16)


def dot(a, b, dims=((1,), (0,))):
    return lax.dot_general(a, b, (dims, ((), ())), preferred_element_type=F32)


def kernel(ids_ref, slots_ref, gates_ref, grad_hbm, hid_hbm, w_hbm, hout, wout,
           arr, outg, grad, hid, w, hmain, htail, utail, acc, sec,
           in_sem, send_sem, recv_sem, hsend_sem, hrecv_sem):
    section = lax.axis_index("section")
    z = lax.axis_index("dp")
    xy = lax.axis_index("expert")
    x, yh = lax.div(xy, 2), lax.rem(xy, 2)
    zb = lax.rem(z, 2)
    e = lax.div(z, 2)
    sg = 2 * zb - 1

    grad_in = pltpu.make_async_copy(grad_hbm, grad, in_sem.at[0])
    grad_in.start()
    hid_in = pltpu.make_async_copy(hid_hbm, hid, in_sem.at[1])
    hid_in.start()
    w_in = pltpu.make_async_copy(w_hbm, w, in_sem.at[2])
    w_in.start()

    def device(dz, dx, flip, ds=0):
        to_y = 1 - yh if flip else yh
        return (section + ds, lax.rem(z + dz + 8, 8), lax.rem(x + dx + 4, 4) * 2 + to_y)

    zflip = 1 - 2 * zb
    to_z = device(zflip, 0, False)
    to_y = device(0, 0, True)
    to_right = device(0, 1, False)
    to_left = device(0, -1, False)
    transit = {1: device(sg, 0, False), 2: device(-2 * sg, 0, False), 3: device(3 * sg, 0, False)}
    transit_from = {1: transit[1], 2: device(2 * sg, 0, False), 3: transit[3]}

    barrier = pltpu.get_barrier_semaphore()
    after = (lax.rem(section + 1, 4), z, xy)
    for other in (to_z, to_y, to_right, to_left, transit_from[1], transit_from[2], transit_from[3], after):
        pl.semaphore_signal(barrier, inc=1, device_id=other, device_id_type=MESH)

    def chunk_expert(j):
        return lax.rem(e + {0: 0, 1: sg, 2: -sg, 3: 2}[j] + 4, 4)

    experts = [chunk_expert(j) for j in range(4)]

    def expert_rows(j):
        base = jnp.full(j.shape, experts[3] * CAP, I32)
        for k in (2, 1, 0):
            base = jnp.where(j == k, experts[k] * CAP, base)
        return base

    def slot_of(j, dx=0, fy=False, fz=False):
        tz = z + zflip if fz else z
        tsg = -sg if fz else sg
        ty = 1 - yh if fy else yh
        return lax.rem(tz + tsg * j + 8, 8) * PLANE + lax.rem(x + dx + 4, 4) * 2 + ty

    place = ids_ref[...] * CAP + slots_ref[...]
    place0, place1 = place[0:1, :], place[1:2, :]
    gate0, gate1 = gates_ref[0:1, :], gates_ref[1:2, :]
    mine = slot_of(0)

    def match(want):
        hit0, hit1 = place0 == want, place1 == want
        gate = jnp.sum(jnp.where(hit0, gate0, 0.0) + jnp.where(hit1, gate1, 0.0), axis=1, keepdims=True)
        return hit0 | hit1, gate

    def pack(rounds):
        n = len(rounds)
        targets = [arr.at[mine] if j == 0 else outg.at[j - 1] for j in rounds]
        m = iota((BAND * n, 1), 0)
        base = expert_rows((m >> 4) + rounds[0])
        for h in range(2):
            hit, gate = match(base + BAND * h + (m & 15))
            pick = onehot(hit)
            for c in range(0, D, 512):
                part = (dot(pick, grad[:, c:c + 512]) * gate).astype(BF16)
                for k in range(n):
                    targets[k][:, h * D + c:h * D + c + 512] = part[BAND * k:BAND * (k + 1)]
        hit, gate = match(base + 2 * BAND + (m & 3))
        part = jnp.zeros((BAND * n, QUARTER), F32)
        for q in range(4):
            part += dot(onehot(hit & (((m >> 2) & 3) == q)), grad[:, q * QUARTER:(q + 1) * QUARTER])
        part = (part * gate).astype(BF16)
        for k in range(n):
            targets[k][:, 2 * D:WIDTH] = part[BAND * k:BAND * (k + 1)]

    grad_in.wait()
    pack((0,))
    pl.semaphore_wait(barrier, 8)

    sends = []
    lanes = {name: [] for name in WINDOW}
    seen = set()
    count = iter(range(160))

    def copy_of(place, cols, to, n):
        piece = arr.at[slot_of(*place), :, pl.ds(cols[0], cols[1])]
        return pltpu.make_async_remote_copy(
            src_ref=piece, dst_ref=piece, send_sem=send_sem.at[n],
            recv_sem=recv_sem.at[slot_of(*place), SEM_OF[cols]], device_id=to, device_id_type=MESH)

    def start(copy, lane):
        queue = lanes[lane]
        if len(queue) >= WINDOW[lane]:
            queue.pop(0).wait_send()
        copy.start()
        queue.append(copy)

    def send(place, cols, to, lane):
        start(copy_of(place, cols, to, next(count)), lane)

    def send_transit(j):
        start(pltpu.make_async_remote_copy(
            src_ref=outg.at[j - 1], dst_ref=arr.at[mine], send_sem=send_sem.at[next(count)],
            recv_sem=recv_sem.at[mine, 0], device_id=transit[j], device_id_type=MESH), "T")

    def need(j, dx=0, fy=False, fz=False, cols=None):
        dx = dx % 4
        if (dx, fy, fz) == (0, 0, 0):
            parts = [(0, WIDTH)] if j else []
        elif cols == A_ALL and dx == 2:
            parts = [A_0, A_1]
        elif cols == B_ALL and (dx, fy, fz) == (2, 0, 0):
            parts = [B_0, B_1]
        else:
            parts = [cols]
        for part in parts:
            if (j, dx, fy, fz, part) not in seen:
                seen.add((j, dx, fy, fz, part))
                copy_of((j, dx, fy, fz), part, to_z, 0).wait_recv()

    def issue(name, j=0, *rest):
        if name[0] == "T":
            send_transit(int(name[1]))
        elif name == "A1":
            need(j)
            if j in Y_FIRST:
                send((j,), A_ALL, to_y, "y")
            else:
                send((j,), A_ALL, to_z, "zp")
        elif name == "A2" and j in Y_FIRST:
            need(j, 0, rest[0], False, A_ALL)
            send((j, 0, rest[0], False), A_ALL, to_z, "zp")
        elif name == "A2":
            need(j, 0, False, rest[0], A_ALL)
            send((j, 0, False, rest[0]), A_ALL, to_y, "y")
        elif name in ("A3R", "A3L"):
            need(j, 0, *rest, A_ALL)
            to, lane = (to_right, "xr") if name == "A3R" else (to_left, "xl")
            send((j, 0, *rest), A_ALL, to, lane)
        elif name == "A4R":
            need(j, -1, *rest, A_ALL)
            send((j, -1, *rest), A_0, to_right, "xr")
        elif name == "A4L":
            need(j, 1, *rest, A_ALL)
            send((j, 1, *rest), A_1, to_left, "xl")
        elif name in ("B1R", "B1L"):
            need(j)
            to, lane = (to_right, "xr") if name == "B1R" else (to_left, "xl")
            send((j,), B_ALL, to, lane)
        elif name == "B2R":
            need(j, -1, False, False, B_ALL)
            send((j, -1), B_0, to_right, "xr")
        elif name == "B2L":
            need(j, 1, False, False, B_ALL)
            send((j, 1), B_1, to_left, "xl")
        else:
            dx = rest[0]
            z_first = (j, dx % 4) in Z_FIRST
            other = len(rest) > 1 and rest[1]
            place = (j, dx, False, other) if z_first else (j, dx, other, False)
            need(*place, B_ALL)
            if (name == "B3") == z_first:
                send(place, B_ALL, to_z, "zp")
            else:
                send(place, B_ALL, to_y, "y")

    def need_plane(j, fz, far):
        for fy in (False, True):
            for dx in (0, 1, 3, 2) if far else (0, 1, 3):
                need(j, dx, fy, fz, A_ALL)
                need(j, dx, fy, fz, B_ALL)

    v = iota((1, MAIN), 1)
    main_at = CAP * ((v >> 4) & 7) + BAND * (v >> 7) + (v & 15)
    perm_main = onehot(iota((ROWS, 1), 0) == main_at)
    u = iota((1, 128), 1)
    tail_at = CAP * ((u & 31) >> 2) + 2 * BAND + (u & 3)
    tail_match = iota((ROWS, 1), 0) == tail_at
    perm_tail = onehot(iota((ROWS, 1), 0) == tail_at)[:, 0:TAILS]

    def turn_hidden(b):
        rows = hid[ROWS * b:ROWS * b + ROWS, :]
        hmain[b] = dot(rows, perm_main, ((0,), (0,))).astype(BF16)
        spread = onehot(tail_match & ((u >> 5) == b % 4))
        part = dot(rows, spread, ((0,), (0,))).astype(BF16)
        cols = slice(128 * (b // 4), 128 * (b // 4) + 128)
        if b % 4 == 0:
            htail[:, cols] = part
        else:
            htail[:, cols] += part

    def perms(sources):
        at = iota((sources * CAP, 1), 0)
        p = iota((1, sources * 2 * BAND), 1)
        main = onehot(at == CAP * ((p >> 4) & (sources - 1)) + BAND * (p >> (4 + sources.bit_length() - 1)) + (p & 15))
        q = iota((1, 128), 1)
        tail = onehot(at == CAP * (q >> 2) + 2 * BAND + (q & 3))[:, 0:sources * TAIL]
        return main, tail

    perms_whole, perms_half = perms(PLANE), perms(PLANE // 2)

    def unpack_tails(start, sources):
        packed = arr[pl.ds(start, sources), :, 2 * D:WIDTH].reshape(sources * BAND, QUARTER)
        t = iota((sources * TAIL, 1), 0)
        v = iota((1, sources * BAND), 1)
        rows = pl.ds(pl.multiple_of(start * TAIL, BAND), sources * TAIL)
        for q in range(4):
            pick = onehot(v == BAND * (t >> 2) + 4 * q + (t & 3))
            utail[rows, q * QUARTER:(q + 1) * QUARTER] = dot(pick, packed).astype(BF16)

    def band(b, h, c, n):
        return arr[pl.ds(PLANE * b, PLANE), :, h * D + c:h * D + c + n].reshape(PLANE * BAND, n)

    def hidden_copy(b, side, at, rows):
        piece = pl.ds(pl.multiple_of(at, BAND), rows)
        return pltpu.make_async_remote_copy(
            src_ref=sec.at[piece], dst_ref=hout.at[piece], send_sem=hsend_sem.at[b, side],
            recv_sem=hrecv_sem.at[b, side], device_id=device(0, 0, False, -1), device_id_type=MESH)

    def pair_of(side):
        near = lax.div(x, 2)
        return 1 - near if side else near

    def plane_at(plane):
        return lax.div(slot_of(plane[0], 0, False, plane[1]), PLANE)

    def hidden_copies(plane, sides=(0, 1)):
        b = plane_at(plane)
        if plane in SPLIT:
            return [hidden_copy(b, side, b * ROWS + pair_of(side) * (ROWS // 2), ROWS // 2) for side in sides]
        return [hidden_copy(b, 0, b * ROWS, ROWS)]

    def section_part(b, start, sources, perms):
        mains, tails = sources * 2 * BAND, sources * TAIL
        rows = jnp.concatenate(
            [arr[pl.ds(start, sources), :, 0:D].reshape(mains // 2, D),
             arr[pl.ds(start, sources), :, D:2 * D].reshape(mains // 2, D),
             utail[pl.ds(pl.multiple_of(start * TAIL, BAND), tails), :]], axis=0)
        out = dot(rows, w[...], ((1,), (1,))).astype(BF16)
        out = dot(perms[0], out[0:mains]) + dot(perms[1], out[mains:])
        sec[pl.ds(pl.multiple_of(start * CAP, BAND), sources * CAP), :] = out.astype(BF16)

    def weight_part(b, c, n, first, last):
        rows = jnp.concatenate([band(b, 0, c, n), band(b, 1, c, n)], axis=0)
        part = dot(hmain[b], rows)
        if not first:
            part += acc[:, c:c + n]
        if not last:
            acc[:, c:c + n] = part
        else:
            part += dot(htail[...], utail[:, c:c + n])
            wout[:, c:c + n] = part.astype(BF16)

    def compute(j, fz, piece):
        plane = (j, bool(fz))
        b = plane_at(plane)
        sections = 2 if plane in SPLIT else 1
        if piece < sections:
            need_plane(*plane, far=piece == sections - 1)
            start = b * PLANE
            if sections == 2:
                start = start + pair_of(piece) * (PLANE // 2)
            unpack_tails(start, PLANE // sections)

            @pl.when(section > 0)
            def _():
                section_part(b, start, PLANE // sections, perms_half if sections == 2 else perms_whole)
                hidden_copies(plane, (piece,))[0].start()
        else:
            for c in (0, 512):
                at = (piece - sections) * 1024 + c
                weight_part(b, at, 512, plane == planes[0], plane == planes[-1])

    planes = [(step[1], bool(step[2])) for step in ORDER if step[0] == "C" and step[3] == 0]
    for step in ORDER:
        if step[0] == "H":
            if step[1] == 0:
                hid_in.wait()
            turn_hidden(step[1])
        elif step[0] == "C":
            if step[1:3] == planes[0] and step[3] == 0:
                w_in.wait()
            compute(*step[1:])
        else:
            if step == ("T1",):
                pack((1, 2, 3))
            issue(*step)
    for queue in lanes.values():
        sends.extend(queue)

    @pl.when(section == 3)
    def _():
        hout[...] = jnp.zeros((SLOTS, UNITS), BF16)

    for copy in sends:
        copy.wait_send()

    @pl.when(section > 0)
    def _():
        for plane in planes:
            for copy in hidden_copies(plane):
                copy.wait_send()

    @pl.when(section < 3)
    def _():
        for plane in planes:
            for copy in hidden_copies(plane):
                copy.wait_recv()


def body(grad_out, expert_ids, slot_ids, gates, hidden, w_down):
    anywhere = pl.BlockSpec(memory_space=pl.ANY)
    vmem = pl.BlockSpec(memory_space=pltpu.VMEM)
    dma = pltpu.SemaphoreType.DMA
    hout, wout = pl.pallas_call(
        kernel,
        out_shape=(pltpu.VMEM((SLOTS, UNITS), BF16), pltpu.VMEM((UNITS, D), BF16)),
        in_specs=[vmem] * 3 + [anywhere] * 3,
        out_specs=(vmem, vmem),
        scratch_shapes=[
            pltpu.VMEM((BLOCKS * PLANE, BAND, WIDTH), BF16),
            pltpu.VMEM((3, BAND, WIDTH), BF16),
            pltpu.VMEM((128, D), BF16),
            pltpu.VMEM((SLOTS, UNITS), BF16),
            pltpu.VMEM((UNITS, D), BF16),
            pltpu.VMEM((BLOCKS, UNITS, MAIN), BF16),
            pltpu.VMEM((UNITS, BLOCKS * TAILS), BF16),
            pltpu.VMEM((BLOCKS * TAILS, D), BF16),
            pltpu.VMEM((UNITS, D), F32),
            pltpu.VMEM((SLOTS, UNITS), BF16),
            dma((3,)), dma((160,)), dma((64, 4)), dma((8, 2)), dma((8, 2)),
        ],
        compiler_params=pltpu.CompilerParams(
            collective_id=0, has_side_effects=True, vmem_limit_bytes=54 * 2**20),
        cost_estimate=pl.CostEstimate(flops=15 * 10**9, bytes_accessed=12 * 10**6, transcendentals=0),
        name="dispatch_and_products",
    )(expert_ids[0].T, slot_ids[0].T, gates[0].T, grad_out[0], hidden[0], w_down[0])
    return (hout[None], wout[None])


def solution(mesh):
    in_specs = (
        P("section", ("dp", "expert"), None),
        P("section", ("dp", "expert"), None),
        P("section", ("dp", "expert"), None),
        P("section", ("dp", "expert"), None),
        P("section", None, ("dp", "expert")),
        P("section", ("dp", "expert"), None),
    )
    out_specs = (P("section", None, ("dp", "expert")), P("section", ("dp", "expert"), None))
    return jax.shard_map(body, mesh=mesh, in_specs=in_specs, out_specs=out_specs, check_vma=False)
```
